128 devices in a mesh: expert: 4 (over y), dp: 32 (over z, x, core).
Axes of the slice: x: 4, y: 4, z: 4, core: 2. Of those that a mesh axis runs over, the one named last changes fastest.
Arguments:
- tokens: bfloat16 [4096, 2048], P(('expert', 'dp')), may hold values from -6 to 6
- expert_ids: int32 [4096, 6], P(('expert', 'dp')), may hold values from 0 to 63, all different within a row; in each aligned block of 32 rows (0 to 31, 32 to 63, ...) at most 4 rows name the same one
- gate_weights: float32 [4096, 6], P(('expert', 'dp')), may hold values from 0.1 to 1
- cotangent: bfloat16 [4096, 2048], P(('expert', 'dp')), may hold values from -6 to 6
- w_gate: bfloat16 [128, 2048, 704], P(('expert', 'dp')), may hold values from -0.125 to 0.125
- w_up: bfloat16 [128, 2048, 704], P(('expert', 'dp')), may hold values from -0.125 to 0.125
- w_down: bfloat16 [128, 704, 2048], P(('expert', 'dp')), may hold values from -0.15625 to 0.15625
Outputs:
- mixed: bfloat16 [4096, 2048], P(('expert', 'dp'))
- d_tokens: bfloat16 [4096, 2048], P(('expert', 'dp'))
- d_gates: float32 [4096, 6], P(('expert', 'dp'))
- g_gate: bfloat16 [128, 2048, 704], P(('expert', 'dp'))
- g_up: bfloat16 [128, 2048, 704], P(('expert', 'dp'))
- g_down: bfloat16 [128, 704, 2048], P(('expert', 'dp'))
The draws below stay inside these ranges and needn't reach their ends.
Inputs may be any that keep to these rules, and one draw needn't show every extreme that they name: `expert_ids`: within the 32 tokens of one device, each token names 6 different experts, and no expert is named by more than 4 of these tokens; in every draw some device fills some expert's 4 slots.
All inputs are finite; a program needn't handle non-finite values.
Results may differ from the reference program's by a relative error of at most 0.0064.
Values may be sent and summed in bfloat16 or wider, within the bound.
No kernel may reach another device: no remote copies, remote signals or barrier semaphores. Data moves between devices by JAX's collectives and lax.ppermute only.
A program may use at most 128 MiB of HBM per device.

```python
import math
import jax
import jax.numpy as jnp
import numpy as np
from jax import lax

D = 2048
HID = 1408
TOP = 6
TOK_DEV = 32
EXPERTS = 64
HALF_HID = 704
CAP = 4
TOKENS = 4096
DEVICES = 128


def block_levels(rng, extent, split, smallest, top_value):
    level, own = 1.0, jax.random.fold_in(rng, 6)
    for axis_at, shards_of in split:
        draws = jnp.exp(jax.random.uniform(jax.random.fold_in(own, axis_at), (shards_of,), jnp.float32, smallest / len(split), top_value / len(split)))
        level = level * jnp.repeat(draws, extent[axis_at] // shards_of).reshape([-1 if axis == axis_at else 1 for axis in range(len(extent))])
    return level


def shared_out(key, own, number, rows, count, top, limit, slope):
    order = jax.random.permutation(key, count)
    heavy_load, common = shares(count, rows * top, limit, slope, True), shares(count, rows * top, limit, slope, False)
    places = jnp.arange(count)

    def named(lengths, rotation):
        used = int((lengths > 0).sum())
        fixed = max(1, used // 4)
        passed = fixed + (places - fixed + rotation * (used - fixed)) % max(1, count - fixed)
        return jnp.zeros((count,), jnp.int32).at[order[jnp.where(places < fixed, places, passed)]].set(jnp.asarray(lengths, jnp.int32))

    lengths = jnp.where(number % 4 == 0, named(heavy_load, number // 4), named(common, number - number // 4 - 1))
    mixed = jax.random.permutation(jax.random.fold_in(own, 3), count)
    giver, sink = mixed[0:count // 2 * 2:2], mixed[1:count // 2 * 2:2]
    room = jnp.minimum(lengths[giver] - 1, limit - lengths[sink]) // 2
    room = jnp.where((giver == order[0]) | (sink == order[0]) | (lengths[sink] == 0), 0, jnp.maximum(room, 0))
    passed = jax.random.randint(jax.random.fold_in(own, 4), (count // 2,), 0, 1 << 20) % (room + 1)
    lengths = lengths.at[giver].add(-passed).at[sink].add(passed)
    members = jnp.searchsorted(jnp.cumsum(lengths), jnp.arange(rows * top), side="right").astype(jnp.int32)
    table = members.reshape(top, rows).T
    table = table[jax.random.permutation(jax.random.fold_in(own, 1), rows)]
    rotation = jax.random.randint(jax.random.fold_in(own, 2), (rows, 1), 0, top)
    return jnp.take_along_axis(table, (jnp.arange(top)[None, :] + rotation) % top, axis=1)


def shares(number_of, total, reach, skew, full):
    portions = [(1 << 20) // math.isqrt(rank ** skew) + 1 for rank in range(1, number_of + 1)]
    largest = reach if full else min(reach, max(-(-total // number_of), total * portions[0] // sum(portions)))
    least = 1 if total - largest >= number_of - 1 else 0
    given, spare = [largest] + [least] * (number_of - 1), total - largest - least * (number_of - 1)
    while spare > 0:
        candidates = [i for i in range(1, number_of) if given[i] < largest] or [i for i in range(1, number_of) if given[i] < reach]
        whole, left = sum([portions[i] for i in candidates]), spare
        for i in candidates:
            extra = min(reach - given[i], max(1, left * portions[i] // whole), spare)
            given[i] = given[i] + extra
            spare = spare - extra
    return np.array(given)


def gaussian(own_key, extent, scale, reach, cuts=(), kind=jnp.bfloat16):
    loudness = block_levels(own_key, extent, cuts, -0.22, 0.18) if cuts else 1.0
    values = jax.random.normal(own_key, extent, jnp.float32) * scale * loudness
    return jnp.minimum(jnp.maximum(values, -reach), reach).astype(kind)


def setup_inputs(seed: int = 0) -> dict:
    seeds = jax.random.split(jax.random.key(seed), 8)
    tokens = gaussian(seeds[0], (TOKENS, D), 1.0, 6.0, ((0, 128),))
    expert_ids_keys = jax.random.split(jax.random.fold_in(seeds[1], 1), TOKENS // TOK_DEV)
    expert_ids_turns = jax.random.permutation(jax.random.fold_in(seeds[1], 3), TOKENS // TOK_DEV)
    expert_ids = jax.vmap(lambda own, number: shared_out(jax.random.fold_in(seeds[1], 2), own, number, TOK_DEV, EXPERTS, TOP, CAP, 1))(expert_ids_keys, expert_ids_turns).reshape((TOKENS, TOP))
    gate_weights = jnp.clip(0.1 + 0.9 * jax.random.uniform(seeds[2], (TOKENS, TOP), jnp.float32) ** block_levels(seeds[2], (TOKENS, TOP), ((0, 128),), -0.2, 0.2), 0.1, 1.0)
    cotangent = gaussian(seeds[3], (TOKENS, D), 1.0, 6.0, ((0, 128),))
    w_gate = gaussian(seeds[4], (2 * EXPERTS, D, HALF_HID), D ** -0.5, 0.125, ((0, 128),))
    w_up = gaussian(seeds[5], (2 * EXPERTS, D, HALF_HID), D ** -0.5, 0.125, ((0, 128),))
    w_down = gaussian(seeds[6], (2 * EXPERTS, HALF_HID, D), HID ** -0.5, 0.15625, ((0, 128),))
    return dict(tokens=tokens, expert_ids=expert_ids, gate_weights=gate_weights, cotangent=cotangent, w_gate=w_gate, w_up=w_up, w_down=w_down)


def slots_of(chosen):
    flat_ids = chosen.reshape(-1)
    onehot = (flat_ids[:, None] == jnp.arange(EXPERTS, dtype=jnp.int32)[None, :]).astype(jnp.int32)
    before = jnp.cumsum(onehot, axis=0) - onehot
    return jnp.sum(before * onehot, axis=1).reshape(chosen.shape).astype(jnp.int32)


def expert_pass(x_rows, dy_rows, gate_w, up_w, down_w):
    gate_act = jnp.dot(x_rows, gate_w, preferred_element_type=jnp.float32)
    up_act = jnp.dot(x_rows, up_w, preferred_element_type=jnp.float32)
    sigmoid_gate = jax.nn.sigmoid(gate_act)
    hidden = (gate_act * sigmoid_gate * up_act).astype(jnp.bfloat16)
    partial_out = jnp.dot(hidden, down_w, preferred_element_type=jnp.float32).astype(jnp.bfloat16)
    d_hidden = lax.dot_general(dy_rows, down_w, (((1,), (1,)), ((), ())), preferred_element_type=jnp.float32)
    d_gate = (d_hidden * up_act * sigmoid_gate * (1.0 + gate_act * (1.0 - sigmoid_gate))).astype(jnp.bfloat16)
    d_up = (d_hidden * gate_act * sigmoid_gate).astype(jnp.bfloat16)
    d_rows = lax.dot_general(d_gate, gate_w, (((1,), (1,)), ((), ())), preferred_element_type=jnp.float32)
    d_rows = d_rows + lax.dot_general(d_up, up_w, (((1,), (1,)), ((), ())), preferred_element_type=jnp.float32)
    d_rows = d_rows.astype(jnp.bfloat16)
    grad_gate = lax.dot_general(x_rows, d_gate, (((0,), (0,)), ((), ())), preferred_element_type=jnp.float32).astype(jnp.bfloat16)
    grad_up = lax.dot_general(x_rows, d_up, (((0,), (0,)), ((), ())), preferred_element_type=jnp.float32).astype(jnp.bfloat16)
    grad_down = lax.dot_general(hidden, dy_rows, (((0,), (0,)), ((), ())), preferred_element_type=jnp.float32).astype(jnp.bfloat16)
    return partial_out, d_rows, grad_gate, grad_up, grad_down


def reference(tokens, expert_ids, gate_weights, cotangent, w_gate, w_up, w_down):
    chosen = expert_ids.reshape(DEVICES, TOK_DEV, TOP)
    slot_index = jax.vmap(slots_of)(chosen)
    source = jnp.broadcast_to(jnp.arange(DEVICES, dtype=jnp.int32)[:, None, None], chosen.shape)
    token_rows = jnp.broadcast_to(tokens.reshape(DEVICES, TOK_DEV, 1, D), (DEVICES, TOK_DEV, TOP, D))
    x_buf = jnp.zeros((EXPERTS, DEVICES, CAP, D), jnp.bfloat16).at[chosen, source, slot_index].set(token_rows)
    gates = gate_weights.reshape(DEVICES, TOK_DEV, TOP)
    scaled = (gates[..., None] * cotangent.reshape(DEVICES, TOK_DEV, 1, D).astype(jnp.float32)).astype(jnp.bfloat16)
    dy_buf = jnp.zeros((EXPERTS, DEVICES, CAP, D), jnp.bfloat16).at[chosen, source, slot_index].set(scaled)
    gate_all = w_gate.reshape(EXPERTS, 2, D, HALF_HID)
    up_all = w_up.reshape(EXPERTS, 2, D, HALF_HID)
    down_all = w_down.reshape(EXPERTS, 2, HALF_HID, D)

    def one_expert(inputs):
        x_block, dy_block, gate_e, up_e, down_e = inputs
        x_rows = x_block.reshape(DEVICES * CAP, D)
        dy_rows = dy_block.reshape(DEVICES * CAP, D)
        results = [expert_pass(x_rows, dy_rows, gate_e[half], up_e[half], down_e[half]) for half in range(2)]
        return tuple(jnp.stack([result[member] for result in results]) for member in range(5))

    partial_out, d_rows, grad_gate, grad_up, grad_down = lax.map(one_expert, (x_buf, dy_buf, gate_all, up_all, down_all))
    partial_out = partial_out.reshape(EXPERTS, 2, DEVICES, CAP, D)
    d_rows = d_rows.reshape(EXPERTS, 2, DEVICES, CAP, D)

    def combine(inputs):
        source_dev, chosen_s, slot_s, gate_s, cot_s = inputs
        y_pick = partial_out[chosen_s, :, source_dev, slot_s]
        y_total = y_pick[:, :, 0].astype(jnp.float32) + y_pick[:, :, 1].astype(jnp.float32)
        mixed_s = jnp.sum(gate_s[:, :, None] * y_total, axis=1).astype(jnp.bfloat16)
        dgate_s = jnp.sum(cot_s.astype(jnp.float32)[:, None, :] * y_total, axis=2)
        d_pick = d_rows[chosen_s, :, source_dev, slot_s]
        dtok_s = jnp.sum(d_pick.astype(jnp.float32), axis=(1, 2)).astype(jnp.bfloat16)
        return mixed_s, dgate_s, dtok_s

    mixed, d_gates, d_tokens = lax.map(combine, (jnp.arange(DEVICES, dtype=jnp.int32), chosen, slot_index, gates, cotangent.reshape(DEVICES, TOK_DEV, D)))
    return (mixed.reshape(TOKENS, D), d_tokens.reshape(TOKENS, D), d_gates.reshape(TOKENS, TOP),
            grad_gate.reshape(2 * EXPERTS, D, HALF_HID), grad_up.reshape(2 * EXPERTS, D, HALF_HID),
            grad_down.reshape(2 * EXPERTS, HALF_HID, D))
```

```python
import functools

import jax
import jax.numpy as jnp
from jax import lax
from jax.experimental import pallas as pl
from jax.experimental.pallas import tpu as pltpu
from jax.sharding import Mesh, PartitionSpec as P

BF16, F32, I32 = jnp.bfloat16, jnp.float32, jnp.int32
CAP = 4
NT = (((1,), (1,)), ((), ()))
TN = (((0,), (0,)), ((), ()))
VMEM = pl.BlockSpec(memory_space=pltpu.VMEM)


def mm(a, b, dims=(((1,), (0,)), ((), ()))):
    return lax.dot_general(a, b, dims, preferred_element_type=F32)


def resident(*arrays):
    return [pltpu.with_memory_space_constraint(a, pltpu.VMEM) for a in arrays]


def routing(ids, gates, first, rows):
    top, toks = ids.shape
    r = lax.broadcasted_iota(I32, (rows, toks), 0) + first
    expert, slot, is_dy = r // (2 * CAP), r % CAP, (r // CAP) % 2 == 1
    chosen = jnp.zeros((rows, toks), F32)
    gate = jnp.zeros((rows, toks), F32)
    for k in range(top):
        same = ids[k : k + 1, :] == expert
        chosen = jnp.where(same, 1.0, chosen)
        gate = jnp.where(same, gates[k : k + 1, :], gate)
    earlier = lax.broadcasted_iota(I32, (toks, toks), 0) < lax.broadcasted_iota(I32, (toks, toks), 1)
    before = mm(chosen.astype(BF16), jnp.where(earlier, 1.0, 0.0).astype(BF16))
    fills = (chosen > 0.5) & (jnp.abs(before - slot.astype(F32)) < 0.5)
    return expert, is_dy, fills, gate


def pack_kernel(ids_ref, gates_ref, tok_ref, cot_ref, out_ref):
    rows = out_ref.shape[0]
    _, is_dy, fills, gate = routing(ids_ref[...], gates_ref[...], pl.program_id(0) * rows, rows)
    pick_x = jnp.where(fills & ~is_dy, 1.0, 0.0)
    pick_dy = jnp.where(fills & is_dy, 1.0, 0.0)
    scale = jnp.sum(pick_x + pick_dy * gate, axis=1, keepdims=True)
    values = mm(pick_x.astype(BF16), tok_ref[...]) + mm(pick_dy.astype(BF16), cot_ref[...])
    out_ref[...] = (values * scale).astype(BF16)


def pack(ids, gates, tokens, cot, experts):
    rows, steps = experts * 2 * CAP, 4
    width = tokens.shape[1]
    whole = lambda a: pl.BlockSpec(a.shape, lambda i: (0, 0))
    return pl.pallas_call(
        pack_kernel,
        grid=(steps,),
        in_specs=[whole(ids), whole(gates), whole(tokens), whole(cot)],
        out_specs=pl.BlockSpec((rows // steps, width), lambda i: (i, 0)),
        out_shape=jax.ShapeDtypeStruct((rows, width), BF16),
        name="pack",
    )(ids, gates, tokens, cot)


def deal(size):
    i = lax.broadcasted_iota(I32, (size, size), 0)
    q = lax.broadcasted_iota(I32, (size, size), 1)
    half = size // 2
    r = i % half
    source = (r // CAP) * 2 * CAP + r % CAP + jnp.where(i >= half, CAP, 0)
    return jnp.where(source == q, 1.0, 0.0).astype(BF16)


def hidden_kernel(z_ref, wg_ref, wu_ref, wd_ref, x_ref, dy_ref, h_ref, dg_ref, du_ref):
    part, cols = 256, 512
    rows, width = z_ref.shape
    hid = wg_ref.shape[0]
    perm = deal(part)
    for m in range(rows // part):
        for n in range(width // cols):
            c = slice(n * cols, (n + 1) * cols)
            dealt = mm(perm, z_ref[m * part : (m + 1) * part, c]).astype(BF16)
            x_ref[m * part // 2 : (m + 1) * part // 2, c] = dealt[: part // 2]
            dy_ref[m * part // 2 : (m + 1) * part // 2, c] = dealt[part // 2 :]
    for lo in range(0, hid, 256):
        s = slice(lo, min(lo + 256, hid))
        g = mm(x_ref[...], wg_ref[s, :], NT)
        u = mm(x_ref[...], wu_ref[s, :], NT)
        dh = mm(dy_ref[...], wd_ref[s, :], NT)
        sig = jax.nn.sigmoid(g)
        act = g * sig
        h_ref[:, s] = (act * u).astype(BF16)
        dg_ref[:, s] = (dh * u * sig * (1.0 + g * (1.0 - sig))).astype(BF16)
        du_ref[:, s] = (dh * act).astype(BF16)


def hidden(z, wg, wu, wd):
    rows, width = z.shape[0] // 2, z.shape[1]
    hid = wg.shape[0]
    out = lambda n: pltpu.VMEM((rows, n), BF16)
    return pl.pallas_call(
        hidden_kernel,
        in_specs=[VMEM] * 4,
        out_specs=[VMEM] * 5,
        out_shape=[out(width), out(width), out(hid), out(hid), out(hid)],
        cost_estimate=pl.CostEstimate(
            flops=6 * rows * width * hid, bytes_accessed=rows * width * 8, transcendentals=rows * hid
        ),
        compiler_params=pltpu.CompilerParams(vmem_limit_bytes=24 << 20),
        name="hidden",
    )(*resident(z, wg, wu, wd))


def project_kernel(h_ref, dg_ref, du_ref, wg_ref, wu_ref, wd_ref, out_ref):
    part, cols = 256, 512
    rows, width = out_ref.shape
    back = deal(part)
    for n in range(width // cols):
        c = slice(n * cols, (n + 1) * cols)
        p = mm(h_ref[...], wd_ref[:, c]).astype(BF16)
        q = (mm(dg_ref[...], wg_ref[:, c]) + mm(du_ref[...], wu_ref[:, c])).astype(BF16)
        for m in range(rows // part):
            r = slice(m * part // 2, (m + 1) * part // 2)
            both = jnp.concatenate([p[r], q[r]], axis=0)
            out_ref[m * part : (m + 1) * part, c] = mm(back, both, TN).astype(BF16)


def project(h, dg, du, wg, wu, wd):
    rows, width, hid = h.shape[0], wg.shape[1], h.shape[1]
    return pl.pallas_call(
        project_kernel,
        in_specs=[VMEM] * 6,
        out_specs=VMEM,
        out_shape=pltpu.VMEM((2 * rows, width), BF16),
        cost_estimate=pl.CostEstimate(
            flops=6 * rows * width * hid, bytes_accessed=rows * width * 8, transcendentals=0
        ),
        compiler_params=pltpu.CompilerParams(vmem_limit_bytes=24 << 20),
        name="project",
    )(*resident(h, dg, du, wg, wu, wd))


def weight_grads_kernel(*refs):
    own, other, outs, turned = refs[:5], refs[5:10], refs[10:13], refs[13]
    rows = own[0].shape[0]

    @pl.when(pl.program_id(0) == 0)
    def _():
        for j, part in enumerate((own, other)):
            for i in range(3):
                turned[i, :, j * rows : (j + 1) * rows] = part[2 + i][...].T

    for i, out in ((0, outs[2]), (1, outs[0]), (2, outs[1])):
        side = 1 if i == 0 else 0
        total = mm(turned[i, :, :rows], own[side][...]) + mm(turned[i, :, rows:], other[side][...])
        out[...] = total.astype(BF16)


def weight_grads(own, other):
    rows, width = own[0].shape
    hid = own[2].shape[1]
    cols = 256
    tall = pl.BlockSpec((rows, cols), lambda i: (0, i))
    whole = pl.BlockSpec((rows, hid), lambda i: (0, 0))
    out = pl.BlockSpec((hid, cols), lambda i: (0, i))
    return pl.pallas_call(
        weight_grads_kernel,
        grid=(width // cols,),
        in_specs=[tall, tall, whole, whole, whole] * 2,
        out_specs=[out] * 3,
        out_shape=[jax.ShapeDtypeStruct((hid, width), BF16)] * 3,
        scratch_shapes=[pltpu.VMEM((3, hid, 2 * rows), BF16)],
        cost_estimate=pl.CostEstimate(
            flops=12 * rows * width * hid, bytes_accessed=6 * hid * width, transcendentals=0
        ),
        compiler_params=pltpu.CompilerParams(vmem_limit_bytes=24 << 20),
        name="weight_grads",
    )(*own, *other)


def combine_kernel(ids_ref, gates_ref, cot_ref, back_ref, mixed_ref, dtok_ref, dgates_ref):
    ids = ids_ref[...]
    rows = back_ref.shape[0]
    expert, is_dy, fills, gate = routing(ids, gates_ref[...], 0, rows)
    gated = jnp.where(fills & ~is_dy, gate, 0.0)
    high = gated.astype(BF16)
    low = (gated - high.astype(F32)).astype(BF16)
    pick = jnp.where(fills & is_dy, 1.0, 0.0).astype(BF16)
    back = back_ref[...]
    mixed_ref[...] = (mm(high, back, TN) + mm(low, back, TN)).astype(BF16)
    dtok_ref[...] = mm(pick, back, TN).astype(BF16)
    inner = jnp.where(fills & ~is_dy, mm(back, cot_ref[...], NT), 0.0)
    for k in range(ids.shape[0]):
        dgates_ref[k : k + 1, :] = jnp.sum(
            jnp.where(ids[k : k + 1, :] == expert, inner, 0.0), axis=0, keepdims=True
        )


def combine(ids, gates, cot, back):
    return pl.pallas_call(
        combine_kernel,
        in_specs=[VMEM] * 4,
        out_specs=[VMEM] * 3,
        out_shape=[
            jax.ShapeDtypeStruct(cot.shape, BF16),
            jax.ShapeDtypeStruct(cot.shape, BF16),
            jax.ShapeDtypeStruct(ids.shape, F32),
        ],
        compiler_params=pltpu.CompilerParams(vmem_limit_bytes=32 << 20),
        name="combine",
    )(ids, gates, cot, *resident(back))


def route(rows):
    chips = lax.axis_size(("expert", "chip"))
    width = rows.shape[1]
    blocks = rows.reshape(chips, -1, width)
    return lax.all_to_all(blocks, ("expert", "chip"), 0, 0, tiled=True).reshape(-1, width)


def swap(rows):
    return lax.ppermute(rows, "core", [(0, 1), (1, 0)])


def local(tokens, expert_ids, gate_weights, cotangent, w_gate, w_up, w_down):
    ids, gates = expert_ids.T, gate_weights.T
    experts = lax.axis_size(("expert", "chip"))
    wg, wu, wd = w_gate[0].T, w_up[0].T, w_down[0]
    z = route(pack(ids, gates, tokens, cotangent, experts))
    z_other = swap(z)
    own = hidden(z, wg, wu, wd)
    other = hidden(z_other, wg, wu, wd)
    theirs = swap(project(*other[2:], wg, wu, wd))
    mine = project(*own[2:], wg, wu, wd)
    back = route((mine.astype(F32) + theirs.astype(F32)).astype(BF16))
    grad_gate, grad_up, grad_down = weight_grads(own, other)
    mixed, d_tokens, d_gates = combine(ids, gates, cotangent, back)
    return (mixed, d_tokens, d_gates.T, grad_gate.T[None], grad_up.T[None], grad_down[None])


def solution(mesh):
    outer, inner = mesh.devices.shape
    chips = Mesh(mesh.devices.reshape(outer, inner // 2, 2), ("expert", "chip", "core"))
    split = ("expert", "chip", "core")
    flat, tall = P(split, None), P(split, None, None)
    return jax.shard_map(
        local,
        mesh=chips,
        in_specs=(flat, flat, flat, flat, tall, tall, tall),
        out_specs=(flat, flat, flat, tall, tall, tall),
        check_vma=False,
    )
```

```python
import functools

import jax
import jax.numpy as jnp
from jax import lax
from jax.experimental import pallas as pl
from jax.experimental.pallas import tpu as pltpu
from jax.sharding import Mesh, PartitionSpec as P

BF16, F32, I32 = jnp.bfloat16, jnp.float32, jnp.int32
CAP = 4
NT = (((1,), (1,)), ((), ()))
TN = (((0,), (0,)), ((), ()))
VMEM = pl.BlockSpec(memory_space=pltpu.VMEM)
HBM = pl.BlockSpec(memory_space=pltpu.HBM)
ANY = pl.BlockSpec(memory_space=pl.ANY)


def mm(a, b, dims=(((1,), (0,)), ((), ()))):
    return lax.dot_general(a, b, dims, preferred_element_type=F32)


def resident(*arrays):
    return [pltpu.with_memory_space_constraint(a, pltpu.VMEM) for a in arrays]


def routing(ids, gates, first, rows):
    top, toks = ids.shape
    r = lax.broadcasted_iota(I32, (rows, toks), 0) + first
    expert, slot, is_dy = r // (2 * CAP), r % CAP, (r // CAP) % 2 == 1
    chosen = jnp.zeros((rows, toks), F32)
    gate = jnp.zeros((rows, toks), F32)
    for k in range(top):
        same = ids[k : k + 1, :] == expert
        chosen = jnp.where(same, 1.0, chosen)
        gate = jnp.where(same, gates[k : k + 1, :], gate)
    earlier = lax.broadcasted_iota(I32, (toks, toks), 0) < lax.broadcasted_iota(I32, (toks, toks), 1)
    before = mm(chosen.astype(BF16), jnp.where(earlier, 1.0, 0.0).astype(BF16))
    fills = (chosen > 0.5) & (jnp.abs(before - slot.astype(F32)) < 0.5)
    return expert, is_dy, fills, gate


def pack_kernel(ids_ref, gates_ref, tok_ref, cot_ref, out_ref):
    rows = out_ref.shape[0]
    _, is_dy, fills, gate = routing(ids_ref[...], gates_ref[...], pl.program_id(0) * rows, rows)
    pick_x = jnp.where(fills & ~is_dy, 1.0, 0.0)
    pick_dy = jnp.where(fills & is_dy, 1.0, 0.0)
    scale = jnp.sum(pick_x + pick_dy * gate, axis=1, keepdims=True)
    pick = jnp.concatenate([pick_x, pick_dy], axis=1).astype(BF16)
    both = jnp.concatenate([tok_ref[...], cot_ref[...]], axis=0)
    out_ref[...] = (mm(pick, both) * scale).astype(BF16)


def pack(ids, gates, tokens, cot, experts):
    rows, steps = experts * 2 * CAP, 4
    width = tokens.shape[1]
    whole = lambda a: pl.BlockSpec(a.shape, lambda i: (0, 0))
    return pl.pallas_call(
        pack_kernel,
        grid=(steps,),
        in_specs=[whole(ids), whole(gates), whole(tokens), whole(cot)],
        out_specs=pl.BlockSpec((rows // steps, width), lambda i: (i, 0)),
        out_shape=jax.ShapeDtypeStruct((rows, width), BF16),
        name="pack",
    )(ids, gates, tokens, cot)


def deal(size):
    i = lax.broadcasted_iota(I32, (size, size), 0)
    q = lax.broadcasted_iota(I32, (size, size), 1)
    half = size // 2
    r = i % half
    source = (r // CAP) * 2 * CAP + r % CAP + jnp.where(i >= half, CAP, 0)
    return jnp.where(source == q, 1.0, 0.0).astype(BF16)


def expert_kernel(z_ref, wg_ref, wu_ref, wd_hbm, wg2_hbm, wu2_hbm, wd2_hbm, *refs):
    rows_hbm, act_hbm, act2_hbm, sent_hbm = refs[:4]
    w, rows_ref, act, sent, w_sem, out_sem = refs[4:]
    part, tile, cols = 256, 352, 1024
    rows, width = z_ref.shape
    hid = wg_ref.shape[0]
    loads = [
        pltpu.make_async_copy(hbm, w.at[i], w_sem.at[i]) for i, hbm in enumerate((wd_hbm, wg2_hbm, wu2_hbm, wd2_hbm))
    ]
    for load in loads:
        load.start()
    perm = deal(part)
    for m in range(rows // part):
        dealt = mm(perm, z_ref[m * part : (m + 1) * part, :]).astype(BF16)
        rows_ref[0, m * part // 2 : (m + 1) * part // 2, :] = dealt[: part // 2]
        rows_ref[1, m * part // 2 : (m + 1) * part // 2, :] = dealt[part // 2 :]
    copies = [pltpu.make_async_copy(rows_ref, rows_hbm, out_sem.at[0])]
    copies[0].start()
    halves = ((wg_ref, wu_ref, w.at[0]), (w.at[1], w.at[2], w.at[3]))
    for h, (wg, wu, wd) in enumerate(halves):
        for load in loads[1:] if h else loads[:1]:
            load.wait()
        for lo in range(0, hid, tile):
            s = slice(lo, lo + tile)
            g = mm(wg[s, :], rows_ref[0], NT)
            u = mm(wu[s, :], rows_ref[0], NT)
            dh = mm(wd[s, :], rows_ref[1], NT)
            sig = jax.nn.sigmoid(g)
            silu = g * sig
            act[h, 0, s, :] = (silu * u).astype(BF16)
            act[h, 1, s, :] = (dh * u * sig * (1.0 + g * (1.0 - sig))).astype(BF16)
            act[h, 2, s, :] = (dh * silu).astype(BF16)
    for h, hbm in enumerate((act_hbm, act2_hbm)):
        copies.append(pltpu.make_async_copy(act.at[h], hbm, out_sem.at[1 + h]))
        copies[-1].start()
    for n in range(width // cols):
        c = slice(n * cols, (n + 1) * cols)
        p = mm(act[0, 0], w[0, :, c], TN) + mm(act[1, 0], w[3, :, c], TN)
        q = mm(act[0, 1], wg_ref[:, c], TN) + mm(act[1, 1], w[1, :, c], TN)
        q = q + mm(act[0, 2], wu_ref[:, c], TN) + mm(act[1, 2], w[2, :, c], TN)
        p, q = p.astype(BF16), q.astype(BF16)
        for m in range(rows // part):
            r = slice(m * part // 2, (m + 1) * part // 2)
            both = jnp.concatenate([p[r], q[r]], axis=0)
            sent[m * part : (m + 1) * part, c] = mm(perm, both, TN).astype(BF16)
        copies.append(pltpu.make_async_copy(sent.at[:, c], sent_hbm.at[:, c], out_sem.at[3 + n]))
        copies[-1].start()
    for copy in copies:
        copy.wait()


def expert(z, mine, theirs):
    rows, width = z.shape[0] // 2, z.shape[1]
    hid = mine[0].shape[0]
    out = lambda *n: pltpu.HBM(n, BF16)
    return pl.pallas_call(
        expert_kernel,
        in_specs=[VMEM] * 3 + [HBM] + [ANY] * 3,
        out_specs=[HBM] * 4,
        out_shape=[out(2, rows, width), out(3, hid, rows), out(3, hid, rows), out(2 * rows, width)],
        scratch_shapes=[
            pltpu.VMEM((4, hid, width), BF16),
            pltpu.VMEM((2, rows, width), BF16),
            pltpu.VMEM((2, 3, hid, rows), BF16),
            pltpu.VMEM((2 * rows, width), BF16),
            pltpu.SemaphoreType.DMA((4,)),
            pltpu.SemaphoreType.DMA((5,)),
        ],
        cost_estimate=pl.CostEstimate(
            flops=24 * rows * width * hid, bytes_accessed=12 * width * hid, transcendentals=2 * rows * hid
        ),
        compiler_params=pltpu.CompilerParams(vmem_limit_bytes=30 << 20),
        name="expert",
    )(*resident(z, *mine[:2]), pltpu.with_memory_space_constraint(mine[2], pltpu.HBM), *theirs)


def weight_grads_kernel(rows_ref, act_ref, rows2_ref, act2_ref, gg_ref, gu_ref, gd_ref):
    for i, side, out in ((0, 1, gd_ref), (1, 0, gg_ref), (2, 0, gu_ref)):
        out[...] = (mm(act_ref[i], rows_ref[side]) + mm(act2_ref[i], rows2_ref[side])).astype(BF16)


def weight_grads(rows, act, rows2, act2):
    _, count, width = rows.shape
    hid = act.shape[1]
    cols = 256
    tall = pl.BlockSpec((2, count, cols), lambda i: (0, 0, i))
    whole = pl.BlockSpec(act.shape, lambda i: (0, 0, 0))
    out = pl.BlockSpec((hid, cols), lambda i: (0, i))
    return pl.pallas_call(
        weight_grads_kernel,
        grid=(width // cols,),
        in_specs=[tall, whole, tall, whole],
        out_specs=[out] * 3,
        out_shape=[jax.ShapeDtypeStruct((hid, width), BF16)] * 3,
        cost_estimate=pl.CostEstimate(
            flops=12 * count * width * hid, bytes_accessed=6 * hid * width, transcendentals=0
        ),
        compiler_params=pltpu.CompilerParams(vmem_limit_bytes=24 << 20),
        name="weight_grads",
    )(rows, act, rows2, act2)


def select_kernel(ids_ref, gates_ref, pick_ref, choice_ref):
    ids = ids_ref[...]
    top, toks = ids.shape
    rows = choice_ref.shape[0]
    expert, is_dy, fills, gate = routing(ids, gates_ref[...], 0, rows)
    gated = jnp.where(fills & ~is_dy, gate, 0.0)
    high = gated.astype(BF16)
    low = (gated - high.astype(F32)).astype(BF16)
    pick = jnp.where(fills & is_dy, 1.0, 0.0).astype(BF16)
    for i, part in enumerate((high, low, pick)):
        pick_ref[i * toks : (i + 1) * toks, :] = part.T
    choice = jnp.full((rows, toks), -1, I32)
    for k in range(top):
        choice = jnp.where(ids[k : k + 1, :] == expert, k, choice)
    choice_ref[...] = jnp.where(fills & ~is_dy, choice, -1)


def select(ids, gates, experts):
    rows, toks = experts * 2 * CAP, ids.shape[1]
    return pl.pallas_call(
        select_kernel,
        in_specs=[VMEM] * 2,
        out_specs=[VMEM] * 2,
        out_shape=[pltpu.VMEM((3 * toks, rows), BF16), pltpu.VMEM((rows, toks), I32)],
        cost_estimate=pl.CostEstimate(flops=rows * toks * 64, bytes_accessed=rows * toks * 10, transcendentals=0),
        name="select",
    )(ids, gates)


def combine_kernel(pick_ref, choice_ref, cot_ref, back_ref, mixed_ref, dtok_ref, dgates_ref):
    toks = cot_ref.shape[0]
    back = back_ref[...]
    sums = mm(pick_ref[...], back)
    mixed_ref[...] = (sums[:toks] + sums[toks : 2 * toks]).astype(BF16)
    dtok_ref[...] = sums[2 * toks :].astype(BF16)
    inner = mm(back, cot_ref[...], NT)
    choice = choice_ref[...]
    for k in range(dgates_ref.shape[0]):
        dgates_ref[k : k + 1, :] = jnp.sum(jnp.where(choice == k, inner, 0.0), axis=0, keepdims=True)


def combine(pick, choice, cot, back, top):
    return pl.pallas_call(
        combine_kernel,
        in_specs=[VMEM] * 4,
        out_specs=[VMEM] * 3,
        out_shape=[
            jax.ShapeDtypeStruct(cot.shape, BF16),
            jax.ShapeDtypeStruct(cot.shape, BF16),
            jax.ShapeDtypeStruct((top, cot.shape[0]), F32),
        ],
        compiler_params=pltpu.CompilerParams(vmem_limit_bytes=32 << 20),
        name="combine",
    )(*resident(pick, choice, cot, back))


def route(rows):
    chips = lax.axis_size(("expert", "chip"))
    width = rows.shape[1]
    blocks = rows.reshape(chips, -1, width)
    return lax.all_to_all(blocks, ("expert", "chip"), 0, 0, tiled=True).reshape(-1, width)


def swap(rows):
    return lax.ppermute(rows, "core", [(0, 1), (1, 0)])


def local(tokens, expert_ids, gate_weights, cotangent, w_gate, w_up, w_down):
    ids, gates = expert_ids.T, gate_weights.T
    experts = lax.axis_size(("expert", "chip"))
    mine = (w_gate[0].T, w_up[0].T, w_down[0])
    theirs = tuple(swap(w) for w in mine)
    z = route(pack(ids, gates, tokens, cotangent, experts))
    rows, act, act_theirs, sent = expert(z, mine, theirs)
    rows2, act2 = swap(rows), swap(act_theirs)
    back = route(sent)
    ids, gates, _ = lax.optimization_barrier((ids, gates, sent[:8, :128]))
    pick, choice = select(ids, gates, experts)
    grads = weight_grads(rows, act, rows2, act2)
    pick, choice, grad_gate, grad_up, grad_down = lax.optimization_barrier((pick, choice, *grads))
    mixed, d_tokens, d_gates = combine(pick, choice, cotangent, back, ids.shape[0])
    return (mixed, d_tokens, d_gates.T, grad_gate.T[None], grad_up.T[None], grad_down[None])


def solution(mesh):
    outer, inner = mesh.devices.shape
    chips = Mesh(mesh.devices.reshape(outer, inner // 2, 2), ("expert", "chip", "core"))
    split = ("expert", "chip", "core")
    flat, tall = P(split, None), P(split, None, None)
    return jax.shard_map(
        local,
        mesh=chips,
        in_specs=(flat, flat, flat, flat, tall, tall, tall),
        out_specs=(flat, flat, flat, tall, tall, tall),
        check_vma=False,
    )
```

```python
import functools

import jax
import jax.numpy as jnp
from jax import lax
from jax.experimental import pallas as pl
from jax.experimental.pallas import tpu as pltpu
from jax.sharding import Mesh, PartitionSpec as P

BF16, F32, I32 = jnp.bfloat16, jnp.float32, jnp.int32
CAP = 4
NT = (((1,), (1,)), ((), ()))
TN = (((0,), (0,)), ((), ()))
VMEM = pl.BlockSpec(memory_space=pltpu.VMEM)
HBM = pl.BlockSpec(memory_space=pltpu.HBM)
ANY = pl.BlockSpec(memory_space=pl.ANY)


def mm(a, b, dims=(((1,), (0,)), ((), ()))):
    return lax.dot_general(a, b, dims, preferred_element_type=F32)


def resident(*arrays):
    return [pltpu.with_memory_space_constraint(a, pltpu.VMEM) for a in arrays]


def routing(ids, gates, first, rows):
    top, toks = ids.shape
    r = lax.broadcasted_iota(I32, (rows, toks), 0) + first
    expert, slot, is_dy = r // (2 * CAP), r % CAP, (r // CAP) % 2 == 1
    chosen = jnp.zeros((rows, toks), F32)
    gate = jnp.zeros((rows, toks), F32)
    for k in range(top):
        same = ids[k : k + 1, :] == expert
        chosen = jnp.where(same, 1.0, chosen)
        gate = jnp.where(same, gates[k : k + 1, :], gate)
    earlier = lax.broadcasted_iota(I32, (toks, toks), 0) < lax.broadcasted_iota(I32, (toks, toks), 1)
    before = mm(chosen.astype(BF16), jnp.where(earlier, 1.0, 0.0).astype(BF16))
    fills = (chosen > 0.5) & (jnp.abs(before - slot.astype(F32)) < 0.5)
    return expert, is_dy, fills, gate


def pack_kernel(ids_hbm, gates_hbm, tok_hbm, cot_hbm, w_hbm, out_hbm, w_ref, *refs):
    ids_ref, gates_ref, both_ref, packed, in_sem, out_sem = refs
    steps = out_sem.shape[0]
    rows, toks = packed.shape[0] // steps, tok_hbm.shape[0]
    pairs = (
        (ids_hbm, ids_ref),
        (gates_hbm, gates_ref),
        (tok_hbm, both_ref.at[:toks]),
        (cot_hbm, both_ref.at[toks:]),
        (w_hbm, w_ref),
    )
    loads = [pltpu.make_async_copy(source, target, in_sem.at[i]) for i, (source, target) in enumerate(pairs)]
    for load in loads:
        load.start()
    for load in loads[:4]:
        load.wait()
    both = both_ref[...]
    copies = []
    for i in range(steps):
        _, is_dy, fills, gate = routing(ids_ref[...], gates_ref[...], i * rows, rows)
        pick_x = jnp.where(fills & ~is_dy, 1.0, 0.0)
        pick_dy = jnp.where(fills & is_dy, 1.0, 0.0)
        scale = jnp.sum(pick_x + pick_dy * gate, axis=1, keepdims=True)
        pick = jnp.concatenate([pick_x, pick_dy], axis=1).astype(BF16)
        s = slice(i * rows, (i + 1) * rows)
        packed[s, :] = (mm(pick, both) * scale).astype(BF16)
        copies.append(pltpu.make_async_copy(packed.at[s], out_hbm.at[s], out_sem.at[i]))
        copies[-1].start()
    for copy in copies:
        copy.wait()
    loads[4].wait()


def pack(ids, gates, tokens, cot, weight, experts):
    rows, width = experts * 2 * CAP, tokens.shape[1]
    return pl.pallas_call(
        pack_kernel,
        in_specs=[HBM] * 5,
        out_specs=[HBM, VMEM],
        out_shape=[pltpu.HBM((rows, width), BF16), pltpu.VMEM(weight.shape, BF16)],
        scratch_shapes=[
            pltpu.VMEM(ids.shape, I32),
            pltpu.VMEM(gates.shape, F32),
            pltpu.VMEM((2 * tokens.shape[0], width), BF16),
            pltpu.VMEM((rows, width), BF16),
            pltpu.SemaphoreType.DMA((5,)),
            pltpu.SemaphoreType.DMA((4,)),
        ],
        cost_estimate=pl.CostEstimate(
            flops=4 * rows * width * ids.shape[1], bytes_accessed=2 * rows * width, transcendentals=0
        ),
        compiler_params=pltpu.CompilerParams(vmem_limit_bytes=12 << 20),
        name="pack",
    )(*(pltpu.with_memory_space_constraint(a, pltpu.HBM) for a in (ids, gates, tokens, cot, weight)))


def deal(size):
    i = lax.broadcasted_iota(I32, (size, size), 0)
    q = lax.broadcasted_iota(I32, (size, size), 1)
    half = size // 2
    r = i % half
    source = (r // CAP) * 2 * CAP + r % CAP + jnp.where(i >= half, CAP, 0)
    return jnp.where(source == q, 1.0, 0.0).astype(BF16)


def expert_kernel(z_ref, wg, wu, wd, wg2, wu2, wd2, rows_hbm, act_hbm, act2_hbm, sent_hbm, *refs):
    rows_ref, act, sent, out_sem = refs
    part, tile, cols = 256, 352, 512
    rows, width = z_ref.shape
    hid = wg.shape[0]
    perm = deal(part)
    for m in range(rows // part):
        dealt = mm(perm, z_ref[m * part : (m + 1) * part, :]).astype(BF16)
        rows_ref[0, m * part // 2 : (m + 1) * part // 2, :] = dealt[: part // 2]
        rows_ref[1, m * part // 2 : (m + 1) * part // 2, :] = dealt[part // 2 :]
    copies = []

    def send(source, target):
        copies.append(pltpu.make_async_copy(source, target, out_sem.at[len(copies)]))
        copies[-1].start()

    send(rows_ref, rows_hbm)
    for h, (wg_h, wu_h, wd_h) in enumerate(((wg, wu, wd), (wg2, wu2, wd2))):
        for lo in range(0, hid, tile):
            s = slice(lo, lo + tile)
            g = mm(wg_h[s, :], rows_ref[0], NT)
            u = mm(wu_h[s, :], rows_ref[0], NT)
            dh = mm(wd_h[s, :], rows_ref[1], NT)
            sig = jax.nn.sigmoid(g)
            silu = g * sig
            act[h, 0, s, :] = (silu * u).astype(BF16)
            act[h, 1, s, :] = (dh * u * (sig + silu * (1.0 - sig))).astype(BF16)
            act[h, 2, s, :] = (dh * silu).astype(BF16)
    send(act.at[0], act_hbm)
    send(act.at[1], act2_hbm)
    for n in range(width // cols):
        c = slice(n * cols, (n + 1) * cols)
        p = mm(act[0, 0], wd[:, c], TN) + mm(act[1, 0], wd2[:, c], TN)
        q = mm(act[0, 1], wg[:, c], TN) + mm(act[1, 1], wg2[:, c], TN)
        q = q + mm(act[0, 2], wu[:, c], TN) + mm(act[1, 2], wu2[:, c], TN)
        p, q = p.astype(BF16), q.astype(BF16)
        for m in range(rows // part):
            r = slice(m * part // 2, (m + 1) * part // 2)
            both = jnp.concatenate([p[r], q[r]], axis=0)
            sent[m * part : (m + 1) * part, c] = mm(perm, both, TN).astype(BF16)
        send(sent.at[:, c], sent_hbm.at[:, c])
    for copy in copies:
        copy.wait()


def expert(z, mine, theirs):
    rows, width = z.shape[0] // 2, z.shape[1]
    hid = mine[0].shape[0]
    out = lambda *n: pltpu.HBM(n, BF16)
    return pl.pallas_call(
        expert_kernel,
        in_specs=[VMEM] * 7,
        out_specs=[HBM] * 4,
        out_shape=[out(2, rows, width), out(3, hid, rows), out(3, hid, rows), out(2 * rows, width)],
        scratch_shapes=[
            pltpu.VMEM((2, rows, width), BF16),
            pltpu.VMEM((2, 3, hid, rows), BF16),
            pltpu.VMEM((2 * rows, width), BF16),
            pltpu.SemaphoreType.DMA((7,)),
        ],
        cost_estimate=pl.CostEstimate(
            flops=24 * rows * width * hid, bytes_accessed=12 * width * hid, transcendentals=2 * rows * hid
        ),
        compiler_params=pltpu.CompilerParams(vmem_limit_bytes=20 << 20),
        name="expert",
    )(*resident(z, *mine, *theirs))


def weight_grads_kernel(rows_ref, act_ref, rows2_ref, act2_ref, gg_ref, gu_ref, gd_ref):
    for i, side, out in ((0, 1, gd_ref), (1, 0, gg_ref), (2, 0, gu_ref)):
        out[...] = (mm(act_ref[i], rows_ref[side]) + mm(act2_ref[i], rows2_ref[side])).astype(BF16)


def weight_grads(rows, act, rows2, act2):
    _, count, width = rows.shape
    hid = act.shape[1]
    cols = 256
    tall = pl.BlockSpec((2, count, cols), lambda i: (0, 0, i))
    whole = pl.BlockSpec(act.shape, lambda i: (0, 0, 0))
    out = pl.BlockSpec((hid, cols), lambda i: (0, i))
    return pl.pallas_call(
        weight_grads_kernel,
        grid=(width // cols,),
        in_specs=[tall, whole, tall, whole],
        out_specs=[out] * 3,
        out_shape=[jax.ShapeDtypeStruct((hid, width), BF16)] * 3,
        cost_estimate=pl.CostEstimate(
            flops=12 * count * width * hid, bytes_accessed=6 * hid * width, transcendentals=0
        ),
        compiler_params=pltpu.CompilerParams(vmem_limit_bytes=24 << 20),
        name="weight_grads",
    )(rows, act, rows2, act2)


def select_kernel(ids_ref, gates_ref, pick_ref, choice_ref):
    ids = ids_ref[...]
    top, toks = ids.shape
    rows = choice_ref.shape[0]
    expert, is_dy, fills, gate = routing(ids, gates_ref[...], 0, rows)
    gated = jnp.where(fills & ~is_dy, gate, 0.0)
    high = gated.astype(BF16)
    low = (gated - high.astype(F32)).astype(BF16)
    pick = jnp.where(fills & is_dy, 1.0, 0.0).astype(BF16)
    for i, part in enumerate((high, low, pick)):
        pick_ref[i * toks : (i + 1) * toks, :] = part.T
    choice = jnp.full((rows, toks), -1, I32)
    for k in range(top):
        choice = jnp.where(ids[k : k + 1, :] == expert, k, choice)
    choice_ref[...] = jnp.where(fills & ~is_dy, choice, -1)


def select(ids, gates, experts):
    rows, toks = experts * 2 * CAP, ids.shape[1]
    return pl.pallas_call(
        select_kernel,
        in_specs=[VMEM] * 2,
        out_specs=[VMEM] * 2,
        out_shape=[pltpu.VMEM((3 * toks, rows), BF16), pltpu.VMEM((rows, toks), I32)],
        cost_estimate=pl.CostEstimate(flops=rows * toks * 64, bytes_accessed=rows * toks * 10, transcendentals=0),
        name="select",
    )(ids, gates)


def combine_kernel(pick_ref, choice_ref, cot_ref, back_ref, mixed_ref, dtok_ref, dgates_ref):
    toks = cot_ref.shape[0]
    back = back_ref[...]
    sums = mm(pick_ref[...], back)
    mixed_ref[...] = (sums[:toks] + sums[toks : 2 * toks]).astype(BF16)
    dtok_ref[...] = sums[2 * toks :].astype(BF16)
    inner = mm(back, cot_ref[...], NT)
    choice = choice_ref[...]
    for k in range(dgates_ref.shape[0]):
        dgates_ref[k : k + 1, :] = jnp.sum(jnp.where(choice == k, inner, 0.0), axis=0, keepdims=True)


def combine(pick, choice, cot, back, top):
    return pl.pallas_call(
        combine_kernel,
        in_specs=[VMEM] * 4,
        out_specs=[VMEM] * 3,
        out_shape=[
            jax.ShapeDtypeStruct(cot.shape, BF16),
            jax.ShapeDtypeStruct(cot.shape, BF16),
            jax.ShapeDtypeStruct((top, cot.shape[0]), F32),
        ],
        compiler_params=pltpu.CompilerParams(vmem_limit_bytes=32 << 20),
        name="combine",
    )(*resident(pick, choice, cot, back))


def route(rows):
    chips = lax.axis_size(("expert", "chip"))
    width = rows.shape[1]
    blocks = rows.reshape(chips, -1, width)
    return lax.all_to_all(blocks, ("expert", "chip"), 0, 0, tiled=True).reshape(-1, width)


def swap(rows):
    return lax.ppermute(rows, "core", [(0, 1), (1, 0)])


def local(tokens, expert_ids, gate_weights, cotangent, w_gate, w_up, w_down):
    ids, gates = expert_ids.T, gate_weights.T
    experts = lax.axis_size(("expert", "chip"))
    mine = (w_gate[0].T, w_up[0].T, w_down[0])
    theirs = tuple(swap(w) for w in mine)
    packed, down = pack(ids, gates, tokens, cotangent, mine[2], experts)
    z = route(packed)
    rows, act, act_theirs, sent = expert(z, (*mine[:2], down), theirs)
    rows2, act2 = swap(rows), swap(act_theirs)
    back = route(sent)
    ids, gates, _ = lax.optimization_barrier((ids, gates, sent[:8, :128]))
    pick, choice = select(ids, gates, experts)
    grads = weight_grads(rows, act, rows2, act2)
    pick, choice, grad_gate, grad_up, grad_down = lax.optimization_barrier((pick, choice, *grads))
    mixed, d_tokens, d_gates = combine(pick, choice, cotangent, back, ids.shape[0])
    return (mixed, d_tokens, d_gates.T, grad_gate.T[None], grad_up.T[None], grad_down[None])


def solution(mesh):
    outer, inner = mesh.devices.shape
    chips = Mesh(mesh.devices.reshape(outer, inner // 2, 2), ("expert", "chip", "core"))
    split = ("expert", "chip", "core")
    flat, tall = P(split, None), P(split, None, None)
    return jax.shard_map(
        local,
        mesh=chips,
        in_specs=(flat, flat, flat, flat, tall, tall, tall),
        out_specs=(flat, flat, flat, tall, tall, tall),
        check_vma=False,
    )
```

```python
import functools

import jax
import jax.numpy as jnp
from jax import lax
from jax.experimental import pallas as pl
from jax.experimental.pallas import tpu as pltpu
from jax.sharding import Mesh, PartitionSpec as P

BF16, F32, I32 = jnp.bfloat16, jnp.float32, jnp.int32
CAP = 4
NT = (((1,), (1,)), ((), ()))
TN = (((0,), (0,)), ((), ()))
VMEM = pl.BlockSpec(memory_space=pltpu.VMEM)
HBM = pl.BlockSpec(memory_space=pltpu.HBM)
ANY = pl.BlockSpec(memory_space=pl.ANY)


def mm(a, b, dims=(((1,), (0,)), ((), ()))):
    return lax.dot_general(a, b, dims, preferred_element_type=F32)


def resident(*arrays):
    return [pltpu.with_memory_space_constraint(a, pltpu.VMEM) for a in arrays]


def routing(ids, gates, first, rows):
    top, toks = ids.shape
    r = lax.broadcasted_iota(I32, (rows, toks), 0) + first
    expert, slot, is_dy = r // (2 * CAP), r % CAP, (r // CAP) % 2 == 1
    chosen = jnp.zeros((rows, toks), F32)
    gate = jnp.zeros((rows, toks), F32)
    for k in range(top):
        same = ids[k : k + 1, :] == expert
        chosen = jnp.where(same, 1.0, chosen)
        gate = jnp.where(same, gates[k : k + 1, :], gate)
    earlier = lax.broadcasted_iota(I32, (toks, toks), 0) < lax.broadcasted_iota(I32, (toks, toks), 1)
    before = mm(chosen.astype(BF16), jnp.where(earlier, 1.0, 0.0).astype(BF16))
    fills = (chosen > 0.5) & (jnp.abs(before - slot.astype(F32)) < 0.5)
    return expert, is_dy, fills, gate


def pack_kernel(ids_hbm, gates_hbm, tok_hbm, cot_hbm, w_hbm, out_ref, w_ref, *refs):
    ids_ref, gates_ref, both_ref, in_sem = refs
    steps = 4
    rows, toks = out_ref.shape[0] // steps, tok_hbm.shape[0]
    pairs = (
        (ids_hbm, ids_ref),
        (gates_hbm, gates_ref),
        (tok_hbm, both_ref.at[:toks]),
        (cot_hbm, both_ref.at[toks:]),
        (w_hbm, w_ref),
    )
    loads = [pltpu.make_async_copy(source, target, in_sem.at[i]) for i, (source, target) in enumerate(pairs)]
    for load in loads:
        load.start()
    for load in loads[:4]:
        load.wait()
    both = both_ref[...]
    for i in range(steps):
        _, is_dy, fills, gate = routing(ids_ref[...], gates_ref[...], i * rows, rows)
        pick_x = jnp.where(fills & ~is_dy, 1.0, 0.0)
        pick_dy = jnp.where(fills & is_dy, 1.0, 0.0)
        scale = jnp.sum(pick_x + pick_dy * gate, axis=1, keepdims=True)
        pick = jnp.concatenate([pick_x, pick_dy], axis=1).astype(BF16)
        out_ref[i * rows : (i + 1) * rows, :] = (mm(pick, both) * scale).astype(BF16)
    loads[4].wait()


def pack(ids, gates, tokens, cot, weight, experts):
    rows, width = experts * 2 * CAP, tokens.shape[1]
    return pl.pallas_call(
        pack_kernel,
        in_specs=[HBM] * 5,
        out_specs=[VMEM, VMEM],
        out_shape=[pltpu.VMEM((rows, width), BF16), pltpu.VMEM(weight.shape, BF16)],
        scratch_shapes=[
            pltpu.VMEM(ids.shape, I32),
            pltpu.VMEM(gates.shape, F32),
            pltpu.VMEM((2 * tokens.shape[0], width), BF16),
            pltpu.SemaphoreType.DMA((5,)),
        ],
        cost_estimate=pl.CostEstimate(
            flops=4 * rows * width * ids.shape[1], bytes_accessed=2 * rows * width, transcendentals=0
        ),
        compiler_params=pltpu.CompilerParams(vmem_limit_bytes=12 << 20),
        name="pack",
    )(*(pltpu.with_memory_space_constraint(a, pltpu.HBM) for a in (ids, gates, tokens, cot, weight)))


def split(both):
    rows, cols = both.shape
    pairs = both.reshape(rows // (4 * CAP), 2, 2 * CAP, cols)
    even, odd = pairs[:, 0], pairs[:, 1]
    first = lax.broadcasted_iota(I32, even.shape, 1) < CAP
    x = jnp.where(first, even, pltpu.roll(odd, CAP, 1))
    dy = jnp.where(first, pltpu.roll(even, CAP, 1), odd)
    return x.reshape(rows // 2, cols), dy.reshape(rows // 2, cols)


def merge(p, q):
    rows, cols = p.shape
    p, q = (a.reshape(rows // (2 * CAP), 2 * CAP, cols) for a in (p, q))
    first = lax.broadcasted_iota(I32, p.shape, 1) < CAP
    even = jnp.where(first, p, pltpu.roll(q, CAP, 1))
    odd = jnp.where(first, pltpu.roll(p, CAP, 1), q)
    return jnp.stack([even, odd], axis=1).reshape(2 * rows, cols)


def expert_kernel(z_ref, wg, wu, wd, wg2, wu2, wd2, rows_hbm, act_hbm, act2_hbm, sent_hbm, *refs):
    rows_ref, act, sent, out_sem = refs
    part, tile, cols = 256, 352, 512
    rows, width = z_ref.shape
    hid = wg.shape[0]
    for m in range(rows // part):
        r = slice(m * part // 2, (m + 1) * part // 2)
        x, dy = split(z_ref[m * part : (m + 1) * part, :].astype(F32))
        rows_ref[0, r, :] = x.astype(BF16)
        rows_ref[1, r, :] = dy.astype(BF16)
    copies = []

    def send(source, target):
        copies.append(pltpu.make_async_copy(source, target, out_sem.at[len(copies)]))
        copies[-1].start()

    send(rows_ref, rows_hbm)
    for h, (wg_h, wu_h, wd_h) in enumerate(((wg, wu, wd), (wg2, wu2, wd2))):
        for lo in range(0, hid, tile):
            s = slice(lo, lo + tile)
            g = mm(wg_h[s, :], rows_ref[0], NT)
            u = mm(wu_h[s, :], rows_ref[0], NT)
            dh = mm(wd_h[s, :], rows_ref[1], NT)
            sig = jax.nn.sigmoid(g)
            silu = g * sig
            act[h, 0, s, :] = (silu * u).astype(BF16)
            act[h, 1, s, :] = (dh * u * (sig + silu * (1.0 - sig))).astype(BF16)
            act[h, 2, s, :] = (dh * silu).astype(BF16)
    send(act.at[0], act_hbm)
    send(act.at[1], act2_hbm)
    for n in range(width // cols):
        c = slice(n * cols, (n + 1) * cols)
        p = mm(act[0, 0], wd[:, c], TN) + mm(act[1, 0], wd2[:, c], TN)
        q = mm(act[0, 1], wg[:, c], TN) + mm(act[1, 1], wg2[:, c], TN)
        q = q + mm(act[0, 2], wu[:, c], TN) + mm(act[1, 2], wu2[:, c], TN)
        sent[:, c] = merge(p, q).astype(BF16)
        send(sent.at[:, c], sent_hbm.at[:, c])
    for copy in copies:
        copy.wait()


def expert(z, mine, theirs):
    rows, width = z.shape[0] // 2, z.shape[1]
    hid = mine[0].shape[0]
    out = lambda *n: pltpu.HBM(n, BF16)
    return pl.pallas_call(
        expert_kernel,
        in_specs=[VMEM] * 7,
        out_specs=[HBM] * 4,
        out_shape=[out(2, rows, width), out(3, hid, rows), out(3, hid, rows), out(2 * rows, width)],
        scratch_shapes=[
            pltpu.VMEM((2, rows, width), BF16),
            pltpu.VMEM((2, 3, hid, rows), BF16),
            pltpu.VMEM((2 * rows, width), BF16),
            pltpu.SemaphoreType.DMA((7,)),
        ],
        cost_estimate=pl.CostEstimate(
            flops=24 * rows * width * hid, bytes_accessed=12 * width * hid, transcendentals=2 * rows * hid
        ),
        compiler_params=pltpu.CompilerParams(vmem_limit_bytes=20 << 20),
        name="expert",
    )(*resident(z, *mine, *theirs))


def weight_grads_kernel(rows_ref, act_ref, rows2_ref, act2_ref, gg_ref, gu_ref, gd_ref):
    for i, side, out in ((0, 1, gd_ref), (1, 0, gg_ref), (2, 0, gu_ref)):
        out[...] = (mm(act_ref[i], rows_ref[side]) + mm(act2_ref[i], rows2_ref[side])).astype(BF16)


def weight_grads(rows, act, rows2, act2):
    _, count, width = rows.shape
    hid = act.shape[1]
    cols = 256
    tall = pl.BlockSpec((2, count, cols), lambda i: (0, 0, i))
    whole = pl.BlockSpec(act.shape, lambda i: (0, 0, 0))
    out = pl.BlockSpec((hid, cols), lambda i: (0, i))
    return pl.pallas_call(
        weight_grads_kernel,
        grid=(width // cols,),
        in_specs=[tall, whole, tall, whole],
        out_specs=[out] * 3,
        out_shape=[jax.ShapeDtypeStruct((hid, width), BF16)] * 3,
        cost_estimate=pl.CostEstimate(
            flops=12 * count * width * hid, bytes_accessed=6 * hid * width, transcendentals=0
        ),
        compiler_params=pltpu.CompilerParams(vmem_limit_bytes=24 << 20),
        name="weight_grads",
    )(rows, act, rows2, act2)


def select_kernel(ids_ref, gates_ref, after_hbm, pick_ref, choice_ref):
    ids = ids_ref[...]
    top, toks = ids.shape
    rows = choice_ref.shape[0]
    expert, is_dy, fills, gate = routing(ids, gates_ref[...], 0, rows)
    gated = jnp.where(fills & ~is_dy, gate, 0.0)
    high = gated.astype(BF16)
    low = (gated - high.astype(F32)).astype(BF16)
    pick = jnp.where(fills & is_dy, 1.0, 0.0).astype(BF16)
    for i, part in enumerate((high, low, pick)):
        pick_ref[i * toks : (i + 1) * toks, :] = part.T
    choice = jnp.full((rows, toks), -1, I32)
    for k in range(top):
        choice = jnp.where(ids[k : k + 1, :] == expert, k, choice)
    choice_ref[...] = jnp.where(fills & ~is_dy, choice, -1)


def select(ids, gates, experts, after):
    rows, toks = experts * 2 * CAP, ids.shape[1]
    return pl.pallas_call(
        select_kernel,
        in_specs=[VMEM] * 2 + [HBM],
        out_specs=[VMEM] * 2,
        out_shape=[pltpu.VMEM((3 * toks, rows), BF16), pltpu.VMEM((rows, toks), I32)],
        cost_estimate=pl.CostEstimate(flops=rows * toks * 64, bytes_accessed=rows * toks * 10, transcendentals=0),
        name="select",
    )(ids, gates, pltpu.with_memory_space_constraint(after, pltpu.HBM))


def combine_kernel(pick_ref, choice_ref, cot_ref, back_ref, mixed_ref, dtok_ref, dgates_ref):
    toks = cot_ref.shape[0]
    back = back_ref[...]
    sums = mm(pick_ref[...], back)
    mixed_ref[...] = (sums[:toks] + sums[toks : 2 * toks]).astype(BF16)
    dtok_ref[...] = sums[2 * toks :].astype(BF16)
    inner = mm(back, cot_ref[...], NT)
    choice = choice_ref[...]
    for k in range(dgates_ref.shape[0]):
        dgates_ref[k : k + 1, :] = jnp.sum(jnp.where(choice == k, inner, 0.0), axis=0, keepdims=True)


def combine(pick, choice, cot, back, top):
    return pl.pallas_call(
        combine_kernel,
        in_specs=[VMEM] * 4,
        out_specs=[VMEM] * 3,
        out_shape=[
            jax.ShapeDtypeStruct(cot.shape, BF16),
            jax.ShapeDtypeStruct(cot.shape, BF16),
            jax.ShapeDtypeStruct((top, cot.shape[0]), F32),
        ],
        compiler_params=pltpu.CompilerParams(vmem_limit_bytes=32 << 20),
        name="combine",
    )(*resident(pick, choice, cot, back))


def route(rows):
    chips = lax.axis_size(("expert", "chip"))
    width = rows.shape[1]
    blocks = rows.reshape(chips, -1, width)
    return lax.all_to_all(blocks, ("expert", "chip"), 0, 0, tiled=True).reshape(-1, width)


def swap(rows):
    return lax.ppermute(rows, "core", [(0, 1), (1, 0)])


def local(tokens, expert_ids, gate_weights, cotangent, w_gate, w_up, w_down):
    ids, gates = expert_ids.T, gate_weights.T
    experts = lax.axis_size(("expert", "chip"))
    mine = (w_gate[0].T, w_up[0].T, w_down[0])
    theirs = tuple(swap(w) for w in mine)
    packed, down = pack(ids, gates, tokens, cotangent, mine[2], experts)
    z = route(packed)
    rows, act, act_theirs, sent = expert(z, (*mine[:2], down), theirs)
    back = route(sent)
    pick, choice = select(ids, gates, experts, sent)
    rows2, act2 = swap(rows), swap(act_theirs)
    grads = weight_grads(rows, act, rows2, act2)
    pick, choice, grad_gate, grad_up, grad_down = lax.optimization_barrier((pick, choice, *grads))
    mixed, d_tokens, d_gates = combine(pick, choice, cotangent, back, ids.shape[0])
    return (mixed, d_tokens, d_gates.T, grad_gate.T[None], grad_up.T[None], grad_down[None])


def solution(mesh):
    outer, inner = mesh.devices.shape
    chips = Mesh(mesh.devices.reshape(outer, inner // 2, 2), ("expert", "chip", "core"))
    split = ("expert", "chip", "core")
    flat, tall = P(split, None), P(split, None, None)
    return jax.shard_map(
        local,
        mesh=chips,
        in_specs=(flat, flat, flat, flat, tall, tall, tall),
        out_specs=(flat, flat, flat, tall, tall, tall),
        check_vma=False,
    )
```

```python
import functools

import jax
import jax.numpy as jnp
from jax import lax
from jax.experimental import pallas as pl
from jax.experimental.pallas import tpu as pltpu
from jax.sharding import Mesh, PartitionSpec as P

BF16, F32, I32 = jnp.bfloat16, jnp.float32, jnp.int32
CAP = 4
NT = (((1,), (1,)), ((), ()))
TN = (((0,), (0,)), ((), ()))
VMEM = pl.BlockSpec(memory_space=pltpu.VMEM)
HBM = pl.BlockSpec(memory_space=pltpu.HBM)
ANY = pl.BlockSpec(memory_space=pl.ANY)


def mm(a, b, dims=(((1,), (0,)), ((), ()))):
    return lax.dot_general(a, b, dims, preferred_element_type=F32)


def resident(*arrays):
    return [pltpu.with_memory_space_constraint(a, pltpu.VMEM) for a in arrays]


def routing(ids, gates, first, rows):
    top, toks = ids.shape
    r = lax.broadcasted_iota(I32, (rows, toks), 0) + first
    expert, slot, is_dy = r // (2 * CAP), r % CAP, (r // CAP) % 2 == 1
    chosen = jnp.zeros((rows, toks), F32)
    gate = jnp.zeros((rows, toks), F32)
    for k in range(top):
        same = ids[k : k + 1, :] == expert
        chosen = jnp.where(same, 1.0, chosen)
        gate = jnp.where(same, gates[k : k + 1, :], gate)
    earlier = lax.broadcasted_iota(I32, (toks, toks), 0) < lax.broadcasted_iota(I32, (toks, toks), 1)
    before = mm(chosen.astype(BF16), jnp.where(earlier, 1.0, 0.0).astype(BF16))
    fills = (chosen > 0.5) & (jnp.abs(before - slot.astype(F32)) < 0.5)
    return expert, is_dy, fills, gate


def pack_kernel(ids_hbm, gates_hbm, tok_hbm, cot_hbm, w_hbm, out_ref, w_ref, *refs):
    ids_ref, gates_ref, both_ref, in_sem = refs
    rows, toks = out_ref.shape[0], tok_hbm.shape[0]
    pairs = (
        (ids_hbm, ids_ref),
        (gates_hbm, gates_ref),
        (tok_hbm, both_ref.at[:toks]),
        (cot_hbm, both_ref.at[toks:]),
        (w_hbm, w_ref),
    )
    loads = [pltpu.make_async_copy(source, target, in_sem.at[i]) for i, (source, target) in enumerate(pairs)]
    for load in loads:
        load.start()
    for load in loads[:4]:
        load.wait()
    _, is_dy, fills, gate = routing(ids_ref[...], gates_ref[...], 0, rows)
    pick_x = jnp.where(fills & ~is_dy, 1.0, 0.0)
    pick_dy = jnp.where(fills & is_dy, 1.0, 0.0)
    scale = jnp.sum(pick_x + pick_dy * gate, axis=1, keepdims=True)
    pick = jnp.concatenate([pick_x, pick_dy], axis=1).astype(BF16)
    out_ref[...] = (mm(pick, both_ref[...]) * scale).astype(BF16)
    loads[4].wait()


def pack(ids, gates, tokens, cot, weight, experts):
    rows, width = experts * 2 * CAP, tokens.shape[1]
    return pl.pallas_call(
        pack_kernel,
        in_specs=[HBM] * 5,
        out_specs=[VMEM, VMEM],
        out_shape=[pltpu.VMEM((rows, width), BF16), pltpu.VMEM(weight.shape, BF16)],
        scratch_shapes=[
            pltpu.VMEM(ids.shape, I32),
            pltpu.VMEM(gates.shape, F32),
            pltpu.VMEM((2 * tokens.shape[0], width), BF16),
            pltpu.SemaphoreType.DMA((5,)),
        ],
        cost_estimate=pl.CostEstimate(
            flops=4 * rows * width * ids.shape[1], bytes_accessed=2 * rows * width, transcendentals=0
        ),
        compiler_params=pltpu.CompilerParams(vmem_limit_bytes=12 << 20),
        name="pack",
    )(*(pltpu.with_memory_space_constraint(a, pltpu.HBM) for a in (ids, gates, tokens, cot, weight)))


def split(both):
    rows, cols = both.shape
    pairs = both.reshape(rows // (4 * CAP), 2, 2 * CAP, cols)
    even, odd = pairs[:, 0], pairs[:, 1]
    first = lax.broadcasted_iota(I32, even.shape, 1) < CAP
    x = jnp.where(first, even, pltpu.roll(odd, CAP, 1))
    dy = jnp.where(first, pltpu.roll(even, CAP, 1), odd)
    return x.reshape(rows // 2, cols), dy.reshape(rows // 2, cols)


def merge(p, q):
    rows, cols = p.shape
    p, q = (a.reshape(rows // (2 * CAP), 2 * CAP, cols) for a in (p, q))
    first = lax.broadcasted_iota(I32, p.shape, 1) < CAP
    even = jnp.where(first, p, pltpu.roll(q, CAP, 1))
    odd = jnp.where(first, pltpu.roll(p, CAP, 1), q)
    return jnp.stack([even, odd], axis=1).reshape(2 * rows, cols)


def expert_kernel(z_ref, wg, wu, wd, wg2, wu2, wd2, rows_hbm, act_hbm, act2_hbm, sent_hbm, *refs):
    rows_ref, act, sent, out_sem = refs
    part, tile, cols = 256, 352, 512
    rows, width = z_ref.shape
    hid = wg.shape[0]
    for m in range(rows // part):
        r = slice(m * part // 2, (m + 1) * part // 2)
        x, dy = split(z_ref[m * part : (m + 1) * part, :].astype(F32))
        rows_ref[0, r, :] = x.astype(BF16)
        rows_ref[1, r, :] = dy.astype(BF16)
    copies = []

    def send(source, target):
        copies.append(pltpu.make_async_copy(source, target, out_sem.at[len(copies)]))
        copies[-1].start()

    send(rows_ref, rows_hbm)
    for h, (wg_h, wu_h, wd_h) in enumerate(((wg, wu, wd), (wg2, wu2, wd2))):
        for lo in range(0, hid, tile):
            s = slice(lo, lo + tile)
            g = mm(wg_h[s, :], rows_ref[0], NT)
            u = mm(wu_h[s, :], rows_ref[0], NT)
            dh = mm(wd_h[s, :], rows_ref[1], NT)
            sig = jax.nn.sigmoid(g)
            silu = g * sig
            act[h, 0, s, :] = (silu * u).astype(BF16)
            act[h, 1, s, :] = (dh * u * (sig + silu * (1.0 - sig))).astype(BF16)
            act[h, 2, s, :] = (dh * silu).astype(BF16)
    send(act.at[0], act_hbm)
    send(act.at[1], act2_hbm)
    for n in range(width // cols):
        c = slice(n * cols, (n + 1) * cols)
        p = mm(act[0, 0], wd[:, c], TN) + mm(act[1, 0], wd2[:, c], TN)
        q = mm(act[0, 1], wg[:, c], TN) + mm(act[1, 1], wg2[:, c], TN)
        q = q + mm(act[0, 2], wu[:, c], TN) + mm(act[1, 2], wu2[:, c], TN)
        sent[:, c] = merge(p, q).astype(BF16)
        send(sent.at[:, c], sent_hbm.at[:, c])
    for copy in copies:
        copy.wait()


def expert(z, mine, theirs):
    rows, width = z.shape[0] // 2, z.shape[1]
    hid = mine[0].shape[0]
    out = lambda *n: pltpu.HBM(n, BF16)
    return pl.pallas_call(
        expert_kernel,
        in_specs=[VMEM] * 7,
        out_specs=[HBM] * 4,
        out_shape=[out(2, rows, width), out(3, hid, rows), out(3, hid, rows), out(2 * rows, width)],
        scratch_shapes=[
            pltpu.VMEM((2, rows, width), BF16),
            pltpu.VMEM((2, 3, hid, rows), BF16),
            pltpu.VMEM((2 * rows, width), BF16),
            pltpu.SemaphoreType.DMA((7,)),
        ],
        cost_estimate=pl.CostEstimate(
            flops=24 * rows * width * hid, bytes_accessed=12 * width * hid, transcendentals=2 * rows * hid
        ),
        compiler_params=pltpu.CompilerParams(vmem_limit_bytes=20 << 20),
        name="expert",
    )(*resident(z, *mine, *theirs))


def weight_grads_kernel(rows_ref, act_ref, rows2_ref, act2_ref, gg_ref, gu_ref, gd_ref):
    for i, side, out in ((0, 1, gd_ref), (1, 0, gg_ref), (2, 0, gu_ref)):
        out[...] = (mm(act_ref[i], rows_ref[side]) + mm(act2_ref[i], rows2_ref[side])).astype(BF16)


def weight_grads(rows, act, rows2, act2):
    _, count, width = rows.shape
    hid = act.shape[1]
    cols = 256
    tall = pl.BlockSpec((2, count, cols), lambda i: (0, 0, i))
    whole = pl.BlockSpec(act.shape, lambda i: (0, 0, 0))
    out = pl.BlockSpec((hid, cols), lambda i: (0, i))
    return pl.pallas_call(
        weight_grads_kernel,
        grid=(width // cols,),
        in_specs=[tall, whole, tall, whole],
        out_specs=[out] * 3,
        out_shape=[jax.ShapeDtypeStruct((hid, width), BF16)] * 3,
        cost_estimate=pl.CostEstimate(
            flops=12 * count * width * hid, bytes_accessed=6 * hid * width, transcendentals=0
        ),
        compiler_params=pltpu.CompilerParams(vmem_limit_bytes=24 << 20),
        name="weight_grads",
    )(rows, act, rows2, act2)


def select_kernel(ids_ref, gates_ref, after_hbm, pick_ref, choice_ref):
    ids = ids_ref[...]
    top, toks = ids.shape
    rows = choice_ref.shape[0]
    expert, is_dy, fills, gate = routing(ids, gates_ref[...], 0, rows)
    gated = jnp.where(fills & ~is_dy, gate, 0.0)
    high = gated.astype(BF16)
    low = (gated - high.astype(F32)).astype(BF16)
    pick = jnp.where(fills & is_dy, 1.0, 0.0).astype(BF16)
    for i, part in enumerate((high, low, pick)):
        pick_ref[i * toks : (i + 1) * toks, :] = part.T
    choice = jnp.full((rows, toks), -1, I32)
    for k in range(top):
        choice = jnp.where(ids[k : k + 1, :] == expert, k, choice)
    choice_ref[...] = jnp.where(fills & ~is_dy, choice, -1)


def select(ids, gates, experts, after):
    rows, toks = experts * 2 * CAP, ids.shape[1]
    return pl.pallas_call(
        select_kernel,
        in_specs=[VMEM] * 2 + [HBM],
        out_specs=[VMEM] * 2,
        out_shape=[pltpu.VMEM((3 * toks, rows), BF16), pltpu.VMEM((rows, toks), I32)],
        cost_estimate=pl.CostEstimate(flops=rows * toks * 64, bytes_accessed=rows * toks * 10, transcendentals=0),
        name="select",
    )(ids, gates, pltpu.with_memory_space_constraint(after, pltpu.HBM))


def combine_kernel(pick_ref, choice_ref, cot_ref, back_ref, mixed_hbm, dtok_hbm, dgates_hbm, out, dgates, sem):
    toks = cot_ref.shape[0]
    back = back_ref[...]
    sums = mm(pick_ref[...], back)
    out[0] = (sums[:toks] + sums[toks : 2 * toks]).astype(BF16)
    out[1] = sums[2 * toks :].astype(BF16)
    pairs = ((out.at[0], mixed_hbm), (out.at[1], dtok_hbm), (dgates, dgates_hbm))
    copies = [pltpu.make_async_copy(source, target, sem.at[i]) for i, (source, target) in enumerate(pairs)]
    for copy in copies[:2]:
        copy.start()
    inner = mm(back, cot_ref[...], NT)
    choice = choice_ref[...]
    for k in range(dgates.shape[0]):
        dgates[k : k + 1, :] = jnp.sum(jnp.where(choice == k, inner, 0.0), axis=0, keepdims=True)
    copies[2].start()
    for copy in copies:
        copy.wait()


def combine(pick, choice, cot, back, top):
    toks, width = cot.shape
    return pl.pallas_call(
        combine_kernel,
        in_specs=[VMEM] * 4,
        out_specs=[HBM] * 3,
        out_shape=[pltpu.HBM((toks, width), BF16), pltpu.HBM((toks, width), BF16), pltpu.HBM((top, toks), F32)],
        scratch_shapes=[
            pltpu.VMEM((2, toks, width), BF16),
            pltpu.VMEM((top, toks), F32),
            pltpu.SemaphoreType.DMA((3,)),
        ],
        compiler_params=pltpu.CompilerParams(vmem_limit_bytes=32 << 20),
        name="combine",
    )(*resident(pick, choice, cot, back))


def route(rows):
    chips = lax.axis_size(("expert", "chip"))
    width = rows.shape[1]
    blocks = rows.reshape(chips, -1, width)
    return lax.all_to_all(blocks, ("expert", "chip"), 0, 0, tiled=True).reshape(-1, width)


def swap(rows):
    return lax.ppermute(rows, "core", [(0, 1), (1, 0)])


def local(tokens, expert_ids, gate_weights, cotangent, w_gate, w_up, w_down):
    ids, gates = expert_ids.T, gate_weights.T
    experts = lax.axis_size(("expert", "chip"))
    mine = (w_gate[0].T, w_up[0].T, w_down[0])
    theirs = tuple(swap(w) for w in mine)
    packed, down = pack(ids, gates, tokens, cotangent, mine[2], experts)
    z = route(packed)
    rows, act, act_theirs, sent = expert(z, (*mine[:2], down), theirs)
    back = route(sent)
    pick, choice = select(ids, gates, experts, sent)
    rows2, act2 = swap(rows), swap(act_theirs)
    grads = weight_grads(rows, act, rows2, act2)
    pick, choice, grad_gate, grad_up, grad_down = lax.optimization_barrier((pick, choice, *grads))
    mixed, d_tokens, d_gates = combine(pick, choice, cotangent, back, ids.shape[0])
    return (mixed, d_tokens, d_gates.T, grad_gate.T[None], grad_up.T[None], grad_down[None])


def solution(mesh):
    outer, inner = mesh.devices.shape
    chips = Mesh(mesh.devices.reshape(outer, inner // 2, 2), ("expert", "chip", "core"))
    split = ("expert", "chip", "core")
    flat, tall = P(split, None), P(split, None, None)
    return jax.shard_map(
        local,
        mesh=chips,
        in_specs=(flat, flat, flat, flat, tall, tall, tall),
        out_specs=(flat, flat, flat, tall, tall, tall),
        check_vma=False,
    )
```
